1024 devices in a mesh: row: 64 (over z, x_lo), col: 16 (over x_hi, y, core).
Axes of the slice: x: 4 (x_hi: 2, x_lo: 2; x = x_hi * 2 + x_lo), y: 4, z: 32, core: 2. Of those that a mesh axis runs over, the one named last changes fastest.
Arguments:
- image_feats: bfloat16 [262144, 768], P(('row', 'col')), may hold values from -24 to 24
- text_emb: bfloat16 [262144, 768], P(('row', 'col')), may hold values from -0.21582031 to 0.21582031
- head_weight: bfloat16 [768, 768], replicated, may hold values from -0.21875 to 0.21875
- partner: int32 [262144], P(('row', 'col')), may hold values from 0 to 262143, as said below
Outputs:
- row_loss: float32 [262144], P(('row', 'col'))
- feat_grad: bfloat16 [262144, 768], P(('row', 'col'))
- text_grad: float32 [262144, 768], P(('row', 'col'))
- head_grad: float32 [768, 768], P('row', 'col')
The draws below stay inside these ranges and needn't reach their ends.
Inputs may be any that keep to these rules, and one draw needn't show every extreme that they name: Each image row's positive text row lies in a text block at loop distance at most 2 from its own block: partner[i] // 256 differs from i // 256 by at most 2 modulo 262144 / 256.
All inputs are finite; a program needn't handle non-finite values.
Results may differ from the reference program's by a relative error of at most 0.017.
Values may be sent and summed in bfloat16 or wider, within the bound.
No kernel may reach another device: no remote copies, remote signals or barrier semaphores. Data moves between devices by JAX's collectives and lax.ppermute only.
A program may use at most 32 MiB of HBM per device.

```python
import jax
import jax.numpy as jnp
from jax import lax

D = 768
ROWS_DEV = 256
HALF = 2
TEXTS = 262144
N_ROW = 64
N_COL = 16


def draw_partner(key, part):
    key = jax.random.fold_in(key, 7)
    first, second = jax.random.split(key)
    blocks = TEXTS // ROWS_DEV
    own = jnp.arange(TEXTS, dtype=jnp.int32) // ROWS_DEV
    offset = jax.random.randint(first, (TEXTS,), -HALF, HALF + 1, dtype=jnp.int32)
    local = jax.random.randint(second, (TEXTS,), 0, ROWS_DEV, dtype=jnp.int32)
    partner = (own + offset) % blocks * ROWS_DEV + local
    partner = partner.at[0].set(0)
    partner = partner.at[TEXTS - 1].set(TEXTS - 1)
    return partner.astype(jnp.int32)


def spiked(array, stream_key, source, target, parts, factor):
    owner, partner = [(jnp.arange(array.shape[axis_at]) // (array.shape[axis_at] // parts)).reshape([-1 if axis == axis_at else 1 for axis in range(array.ndim)]) for axis_at in (source, target)]
    chosen = jax.random.permutation(stream_key, parts)[partner]
    strong = (owner == chosen) | (owner == (partner + parts // 2) % parts)
    return jnp.where(strong, factor * array, array)


def block_levels(rng, shape, cuts, smallest, top_value):
    def one(position, shards_of):
        steps = jax.random.uniform(jax.random.fold_in(jax.random.fold_in(rng, 6), position), (shards_of,), jnp.float32, smallest / len(cuts), top_value / len(cuts))
        return jnp.repeat(jnp.exp(steps), shape[position] // shards_of).reshape((-1,) + (1,) * (len(shape) - position - 1))

    gain = one(*cuts[0])
    for cut in cuts[1:]:
        gain = gain * one(*cut)
    return gain


def bell_draw(rng, shape, spread, most, pieces=(), kind=jnp.bfloat16):
    drawn = spread * jax.random.normal(rng, shape, jnp.float32)
    if pieces:
        drawn = drawn * block_levels(rng, shape, pieces, -0.22, 0.18)
    return jnp.clip(drawn, -most, most).astype(kind)


def bell_draw_with(stream_key, shape, scale, reach, cuts, heavy, held_as=jnp.bfloat16):
    entries = scale * jax.random.normal(stream_key, shape, jnp.float32)
    if cuts:
        entries = entries * block_levels(stream_key, shape, cuts, -0.22, 0.18)
    return jnp.clip(spiked(entries, jax.random.fold_in(stream_key, 3), *heavy), -reach, reach).astype(held_as)


def setup_inputs(seed: int = 0) -> dict:
    arg_keys = jax.random.split(jax.random.key(seed), 5)
    image_feats = bell_draw_with(arg_keys[0], (TEXTS, D), 1.0, 24.0, ((0, 1024),), (0, 1, 256, 6.0))
    text_emb = bell_draw(arg_keys[1], (TEXTS, D), 0.036, 0.21582031, ((0, 1024),))
    head_weight = bell_draw(arg_keys[2], (D, D), D ** -0.5, 0.21875)
    partner = draw_partner(jax.random.fold_in(arg_keys[4], 71), 0)
    return dict(image_feats=image_feats, text_emb=text_emb, head_weight=head_weight, partner=partner)


TEMP = 10.0
BIAS = -4.0

def pair_terms(unit_rows, text_rows, partner_rows, text_block):
    cols = text_block * ROWS_DEV + jnp.arange(ROWS_DEV, dtype=jnp.int32)
    label = jnp.where(partner_rows[:, None] == cols[None, :], 1.0, -1.0).astype(jnp.float32)
    logit = TEMP * jnp.dot(unit_rows, text_rows.T, preferred_element_type=jnp.float32) + BIAS
    loss = lax.optimization_barrier(jnp.sum(jax.nn.softplus(-label * logit), axis=1))
    slope = (-label * jax.nn.sigmoid(-label * logit)).astype(jnp.bfloat16)
    return (loss, slope)

def reference(image_feats, text_emb, head_weight, partner):
    blocks = N_ROW * N_COL
    proj = jnp.dot(image_feats, head_weight, preferred_element_type=jnp.float32)
    norm = jnp.sqrt(lax.optimization_barrier(jnp.sum(proj * proj, axis=1, keepdims=True)) + 1e-06)
    unit = proj / norm
    unit_b = unit.astype(jnp.bfloat16)
    unit_blocks = unit_b.reshape(blocks, ROWS_DEV, D)
    text_blocks = text_emb.reshape(blocks, ROWS_DEV, D)
    partner_blocks = partner.reshape(blocks, ROWS_DEV)
    offsets = jnp.arange(-HALF, HALF + 1, dtype=jnp.int32)

    def image_side(index):
        loss_total = jnp.zeros((ROWS_DEV,), jnp.float32)
        grad_total = jnp.zeros((ROWS_DEV, D), jnp.float32)
        for slot in range(2 * HALF + 1):
            other = ((index + offsets[slot]) % blocks).astype(jnp.int32)
            text_rows = text_blocks[other]
            loss, slope = pair_terms(unit_blocks[index], text_rows, partner_blocks[index], other)
            loss_total = loss_total + loss
            grad_total = grad_total + TEMP * jnp.dot(slope, text_rows, preferred_element_type=jnp.float32)
        return (loss_total, grad_total)

    def text_side(index):
        grad_total = jnp.zeros((ROWS_DEV, D), jnp.float32)
        for slot in range(2 * HALF + 1):
            other = ((index - offsets[slot]) % blocks).astype(jnp.int32)
            loss, slope = pair_terms(unit_blocks[other], text_blocks[index], partner_blocks[other], index)
            grad_total = grad_total + TEMP * jnp.dot(slope.T, unit_blocks[other], preferred_element_type=jnp.float32)
        return grad_total
    indices = jnp.arange(blocks, dtype=jnp.int32)
    row_loss, unit_grad = lax.map(image_side, indices)
    text_grad = lax.map(text_side, indices)
    row_loss = row_loss.reshape(TEXTS)
    unit_grad = unit_grad.reshape(TEXTS, D)
    text_grad = text_grad.reshape(TEXTS, D)
    inner = lax.optimization_barrier(jnp.sum(unit * unit_grad, axis=1, keepdims=True))
    proj_grad = ((unit_grad - unit * inner) / norm).astype(jnp.bfloat16)
    feat_grad = jnp.dot(proj_grad, head_weight.T, preferred_element_type=jnp.float32).astype(jnp.bfloat16)
    head_grad = jnp.dot(image_feats.T, proj_grad, preferred_element_type=jnp.float32)
    return (row_loss, feat_grad, text_grad, head_grad)
```

```python
import jax
import jax.numpy as jnp
from jax import lax
from jax.sharding import PartitionSpec as P

HALF = 2
TEMP = 10.0
BIAS = -4.0
LOOP = ("row", "col")
BF16 = jnp.bfloat16
F32 = jnp.float32


def from_ahead(block, distance):
    n = lax.axis_size(LOOP)
    return lax.ppermute(block, LOOP, [((i + distance) % n, i) for i in range(n)])


def dot(a, b, dims):
    return lax.dot_general(a, b, (dims, ((), ())), preferred_element_type=F32)


def loss_and_slope(logit, match):
    label = jnp.where(match, 1.0, -1.0).astype(F32)
    z = -label * logit
    return jax.nn.softplus(z), (-label * jax.nn.sigmoid(z)).astype(BF16)


def local(image_feats, text_emb, head_weight, partner):
    rows, width = image_feats.shape
    blocks = lax.axis_size(LOOP)
    here = lax.axis_index(LOOP)
    offsets = [o for o in range(-HALF, HALF + 1) if o]

    texts = {o: from_ahead(text_emb, o) for o in sorted(offsets, key=abs, reverse=True)}
    texts[0] = text_emb

    proj = dot(image_feats, head_weight, ((1,), (0,)))
    norm = jnp.sqrt(jnp.sum(proj * proj, axis=1, keepdims=True) + 1e-06)
    unit = proj / norm
    unit_b = unit.astype(BF16)

    place = (partner // rows - here + HALF) % blocks
    within = partner % rows
    codes = jnp.stack([place, within]).astype(BF16)
    parcel = jnp.concatenate([unit_b, jnp.pad(codes, ((0, 14), (0, width - rows)))])
    parcels = {o: from_ahead(parcel, o) for o in sorted(offsets, key=abs, reverse=True)}
    parcels[0] = parcel

    row_loss = jnp.zeros((rows,), F32)
    unit_grad = jnp.zeros(proj.shape, F32)
    column = lax.broadcasted_iota(jnp.int32, (rows, rows), 1)
    for o in (0, -2, 2, -1, 1):
        logit = TEMP * dot(unit_b, texts[o], ((1,), (1,))) + BIAS
        match = (place[:, None] == o + HALF) & (within[:, None] == column)
        loss, slope = loss_and_slope(logit, match)
        row_loss = row_loss + jnp.sum(loss, axis=1)
        unit_grad = unit_grad + TEMP * dot(slope, texts[o], ((1,), (0,)))
    inner = jnp.sum(unit * unit_grad, axis=1, keepdims=True)
    proj_grad = ((unit_grad - unit * inner) / norm).astype(BF16)

    n_col, n_row = lax.axis_size("col"), lax.axis_size("row")
    cols, tall = width // n_col, width // n_row
    terms = dot(proj_grad, image_feats, ((0,), (0,))).astype(BF16)
    mine = lax.all_to_all(terms.reshape(n_col, cols, width), "col", 0, 0, tiled=True)
    pick = jnp.tile(jnp.eye(cols, dtype=BF16), (n_col, 1))
    summed = dot(mine.reshape(width, width), pick, ((0,), (0,))).astype(BF16)
    last = lax.all_to_all(summed.reshape(n_row, 8, tall * cols // 8), "row", 0, 0, tiled=True)
    head_grad = jnp.sum(last.astype(F32), axis=0).reshape(tall, cols)

    feat_grad = dot(proj_grad, head_weight, ((1,), (1,))).astype(BF16)

    text_grad = jnp.zeros(proj.shape, F32)
    line = lax.broadcasted_iota(F32, (rows, rows), 0)
    for o in (0, -2, 2, -1, 1):
        units = parcels[o][:rows]
        info = parcels[o][rows:].astype(F32)
        logit = TEMP * dot(text_emb, units, ((1,), (1,))) + BIAS
        match = (info[0:1, :rows] == HALF - o) & (info[1:2, :rows] == line)
        _, slope = loss_and_slope(logit, match)
        text_grad = text_grad + TEMP * dot(slope, units, ((1,), (0,)))
    return row_loss, feat_grad, text_grad, head_grad


def solution(mesh):
    split = P(LOOP)
    return jax.shard_map(
        local,
        mesh=mesh,
        in_specs=(P(LOOP, None), P(LOOP, None), P(), split),
        out_specs=(split, P(LOOP, None), P(LOOP, None), P("row", "col")),
        check_vma=False,
    )
```

```python
import jax
import jax.numpy as jnp
from jax import lax
from jax.experimental import pallas as pl
from jax.experimental.pallas import tpu as pltpu
from jax.sharding import Mesh, PartitionSpec as P

HALF = 2
TEMP = 10.0
BIAS = -4.0
CORES = 2
TAIL = 16
ROW, CHIP, CORE = "row", "chip", "core"
LOOP = (ROW, CHIP, CORE)
COL = (CHIP, CORE)
BF16 = jnp.bfloat16
F32 = jnp.float32
VMEM = pl.BlockSpec(memory_space=pltpu.VMEM)
SMEM = pl.BlockSpec(memory_space=pltpu.SMEM)


def from_ahead(block, distance):
    n = lax.axis_size(LOOP)
    return lax.ppermute(block, LOOP, [((i + distance) % n, i) for i in range(n)])


def other_core(block):
    return lax.ppermute(block, CORE, [(0, 1), (1, 0)])


def after(value, *earlier):
    return lax.optimization_barrier((value, *earlier))[0]


def dot(a, b, dims):
    return lax.dot_general(a, b, (dims, ((), ())), preferred_element_type=F32)


def kernel_call(body, outs, args, flops, scalars=0):
    moved = sum(a.size * a.dtype.itemsize for a in args)
    moved += sum(o.size * o.dtype.itemsize for o in outs)
    return pl.pallas_call(
        body,
        out_shape=outs,
        in_specs=[SMEM] * scalars + [VMEM] * (len(args) - scalars),
        out_specs=[VMEM] * len(outs),
        compiler_params=pltpu.CompilerParams(vmem_limit_bytes=32 * 2**20),
        cost_estimate=pl.CostEstimate(flops=flops, bytes_accessed=moved, transcendentals=0),
    )(*args)


def prepare(blocks, here_ref, feats_ref, weight_ref, partner_ref, proj_ref, parcel_ref):
    rows, width = feats_ref.shape
    proj = jnp.dot(feats_ref[...], weight_ref[...], preferred_element_type=F32)
    proj_ref[...] = proj
    norm = jnp.sqrt(jnp.sum(proj * proj, axis=1, keepdims=True) + 1e-06)
    parcel_ref[:rows, :] = (proj / norm).astype(BF16)
    partner = partner_ref[...]
    block = lax.div(partner, rows)
    place = block - here_ref[0] + HALF
    place = jnp.where(place < 0, place + blocks, place)
    place = jnp.where(place >= blocks, place - blocks, place)
    line = lax.broadcasted_iota(jnp.int32, (TAIL, rows), 0)
    codes = jnp.where(line == 0, place, jnp.where(line == 1, partner - block * rows, 0))
    parcel_ref[rows:, :] = jnp.zeros((TAIL, width), BF16)
    parcel_ref[rows:, :rows] = codes.astype(F32).astype(BF16)


def pair_terms(text, parcel_ref, place, with_loss=True):
    rows = text.shape[0]
    codes = parcel_ref[rows:, :rows].astype(F32)
    target = (codes[0:1] - (place + HALF)) * rows + codes[1:2]
    match = lax.broadcasted_iota(jnp.int32, (rows, rows), 0).astype(F32) == target
    logit = TEMP * dot(text, parcel_ref[:rows, :], ((1,), (1,))) + BIAS
    z = jnp.where(match, -logit, logit)
    small = jnp.exp(-jnp.abs(z))
    share = 1.0 / (1.0 + small)
    sigmoid = jnp.where(z >= 0, share, small * share)
    slope = jnp.where(match, -sigmoid, sigmoid).astype(BF16)
    if not with_loss:
        return slope
    loss = jnp.sum(jnp.maximum(z, 0.0) + jnp.log1p(small), axis=0, keepdims=True)
    return slope, loss


def image_start(side_ref, parcel_ref, own_ref, mate_ref, ahead_ref, behind_ref, grad_ref, loss_ref):
    side = side_ref[0].astype(F32)
    grad, total = None, None
    for text_ref, place in ((own_ref, 0), (mate_ref, side), (ahead_ref, HALF), (behind_ref, -HALF)):
        text = text_ref[...]
        slope, loss = pair_terms(text, parcel_ref, place)
        part = dot(slope, text, ((0,), (0,)))
        grad, total = (part, loss) if grad is None else (grad + part, total + loss)
    grad_ref[...] = grad
    loss_ref[...] = total


def image_end(
    side_ref, parcel_ref, far_ref, proj_ref, grad_ref, loss_ref, feats_ref, back_ref, terms_ref, out_loss_ref
):
    half = feats_ref.shape[1] // 2
    far = far_ref[...]
    slope, loss = pair_terms(far, parcel_ref, -side_ref[0].astype(F32))
    out_loss_ref[...] = loss_ref[...] + loss
    unit_grad = TEMP * (grad_ref[...] + dot(slope, far, ((0,), (0,))))
    proj = proj_ref[...]
    norm = jnp.sqrt(jnp.sum(proj * proj, axis=1, keepdims=True) + 1e-06)
    unit = proj / norm
    inner = jnp.sum(unit * unit_grad, axis=1, keepdims=True)
    back = ((unit_grad - unit * inner) / norm).astype(BF16)
    back_ref[...] = back
    terms_ref[:, :half] = dot(back, feats_ref[:, half:], ((0,), (0,))).astype(BF16)
    terms_ref[:, half:] = dot(back, feats_ref[:, :half], ((0,), (0,))).astype(BF16)


def text_side(side_ref, text_ref, own_ref, mate_ref, ahead_ref, behind_ref, far_ref, grad_ref):
    rows = text_ref.shape[0]
    side = side_ref[0].astype(F32)
    text = text_ref[...]
    grad = None
    for parcel_ref, place in ((own_ref, 0), (mate_ref, -side), (ahead_ref, -HALF), (behind_ref, HALF), (far_ref, side)):
        slope = pair_terms(text, parcel_ref, place, with_loss=False)
        part = dot(slope, parcel_ref[:rows, :], ((1,), (0,)))
        grad = part if grad is None else grad + part
    grad_ref[...] = TEMP * grad


def local(image_feats, text_emb, head_weight, partner):
    rows, width = image_feats.shape
    blocks = lax.axis_size(LOOP)
    core = lax.axis_index(CORE)
    here = lax.axis_index(LOOP).astype(jnp.int32).reshape(1)
    side = (1 - 2 * core).astype(jnp.int32).reshape(1)
    shape = jax.ShapeDtypeStruct
    product = 2 * rows * width * width
    pair = 2 * rows * rows * width

    ahead, behind = from_ahead(text_emb, HALF), from_ahead(text_emb, -HALF)
    mate = other_core(text_emb)

    proj, parcel = kernel_call(
        lambda *refs: prepare(blocks, *refs),
        [shape((rows, width), F32), shape((rows + TAIL, width), BF16)],
        [here, image_feats, head_weight, partner.reshape(1, rows)],
        product,
        1,
    )
    ahead, behind, parcel = lax.optimization_barrier((ahead, behind, parcel))
    far = other_core(jnp.where(core == 0, ahead, behind))
    grad, loss = kernel_call(
        image_start,
        [shape((rows, width), F32), shape((1, rows), F32)],
        [side, parcel, text_emb, mate, ahead, behind],
        8 * pair,
        1,
    )
    proj_grad, terms, row_loss = kernel_call(
        image_end,
        [shape((rows, width), BF16), shape((width, width), BF16), shape((1, rows), F32)],
        [side, parcel, far, proj, grad, loss, image_feats],
        2 * pair + product,
        1,
    )
    sent = after(parcel, terms)
    parcel_ahead, parcel_behind = from_ahead(sent, HALF), from_ahead(sent, -HALF)
    parcel_mate = other_core(sent)
    parcel_far = other_core(jnp.where(core == 0, parcel_ahead, parcel_behind))

    n_col, n_row = lax.axis_size(COL), lax.axis_size(ROW)
    cols, tall = width // n_col, width // n_row
    mine = lax.all_to_all(terms.reshape(n_col, cols, width), COL, 0, 0, tiled=True)

    (text_grad,) = kernel_call(
        text_side,
        [shape((rows, width), F32)],
        [side, text_emb, parcel, parcel_mate, parcel_ahead, parcel_behind, parcel_far],
        10 * pair,
        1,
    )
    feat_grad = dot(proj_grad, head_weight, ((1,), (1,))).astype(BF16)

    pick = jnp.tile(jnp.eye(cols, dtype=BF16), (n_col, 1))
    summed = dot(mine.reshape(width, width), pick, ((0,), (0,))).astype(BF16)
    order = [(i + n_row // 2) % n_row for i in range(n_row)]
    last = lax.all_to_all(
        summed.reshape(n_row, 8, tall * cols // 8), ROW, 0, 0, axis_index_groups=[order], tiled=True
    )
    head_grad = jnp.sum(last.astype(F32), axis=0).reshape(tall, cols)
    return row_loss.reshape(rows), feat_grad, text_grad, head_grad


def solution(mesh):
    n_row, n_col = mesh.devices.shape
    fine = Mesh(mesh.devices.reshape(n_row, n_col // CORES, CORES), LOOP)
    split = P(LOOP)
    return jax.shard_map(
        local,
        mesh=fine,
        in_specs=(P(LOOP, None), P(LOOP, None), P(), split),
        out_specs=(split, P(LOOP, None), P(LOOP, None), P(ROW, COL)),
        check_vma=False,
    )
```

```python
import jax
import jax.numpy as jnp
from jax import lax
from jax.experimental import pallas as pl
from jax.experimental.pallas import tpu as pltpu
from jax.sharding import Mesh, PartitionSpec as P

HALF = 2
TEMP = 10.0
BIAS = -4.0
CORES = 2
TAIL = 16
ROW, CHIP, CORE = "row", "chip", "core"
LOOP = (ROW, CHIP, CORE)
COL = (CHIP, CORE)
BF16 = jnp.bfloat16
F32 = jnp.float32
VMEM = pl.BlockSpec(memory_space=pltpu.VMEM)
SMEM = pl.BlockSpec(memory_space=pltpu.SMEM)


def from_ahead(block, distance):
    n = lax.axis_size(LOOP)
    return lax.ppermute(block, LOOP, [((i + distance) % n, i) for i in range(n)])


def other_core(block):
    return lax.ppermute(block, CORE, [(0, 1), (1, 0)])


def after(value, *earlier):
    return lax.optimization_barrier((value, *earlier))[0]


def dot(a, b, dims):
    return lax.dot_general(a, b, (dims, ((), ())), preferred_element_type=F32)


def kernel_call(body, outs, args, flops, scalars=0):
    moved = sum(a.size * a.dtype.itemsize for a in args)
    moved += sum(o.size * o.dtype.itemsize for o in outs)
    return pl.pallas_call(
        body,
        out_shape=outs,
        in_specs=[SMEM] * scalars + [VMEM] * (len(args) - scalars),
        out_specs=[VMEM] * len(outs),
        compiler_params=pltpu.CompilerParams(vmem_limit_bytes=32 * 2**20),
        cost_estimate=pl.CostEstimate(flops=flops, bytes_accessed=moved if flops else 0, transcendentals=0),
    )(*args)


def prepare(blocks, here_ref, feats_ref, weight_ref, partner_ref, proj_ref, parcel_ref):
    rows, width = feats_ref.shape
    proj = jnp.dot(feats_ref[...], weight_ref[...], preferred_element_type=F32)
    proj_ref[...] = proj
    norm = jnp.sqrt(jnp.sum(proj * proj, axis=1, keepdims=True) + 1e-06)
    parcel_ref[:rows, :] = (proj / norm).astype(BF16)
    partner = partner_ref[...]
    block = lax.div(partner, rows)
    place = block - here_ref[0] + HALF
    place = jnp.where(place < 0, place + blocks, place)
    place = jnp.where(place >= blocks, place - blocks, place)
    line = lax.broadcasted_iota(jnp.int32, (TAIL, rows), 0)
    codes = jnp.where(line == 0, place, jnp.where(line == 1, partner - block * rows, 0))
    parcel_ref[rows:, :] = jnp.zeros((TAIL, width), BF16)
    parcel_ref[rows:, :rows] = codes.astype(F32).astype(BF16)


def pair_terms(text, parcel, place, with_loss=True):
    rows = text.shape[0]
    codes = parcel[rows:, :rows].astype(F32)
    target = (codes[0:1] - (place + HALF)) * rows + codes[1:2]
    match = lax.broadcasted_iota(jnp.int32, (rows, rows), 0).astype(F32) == target
    logit = TEMP * dot(text, parcel[:rows], ((1,), (1,))) + BIAS
    z = jnp.where(match, -logit, logit)
    small = jnp.exp(-jnp.abs(z))
    share = 1.0 / (1.0 + small)
    sigmoid = jnp.where(z >= 0, share, small * share)
    slope = jnp.where(match, -sigmoid, sigmoid).astype(BF16)
    if not with_loss:
        return slope
    loss = jnp.sum(jnp.maximum(z, 0.0) + jnp.log1p(small), axis=0, keepdims=True)
    return slope, loss


def image_start(side_ref, parcel_ref, own_ref, mate_ref, ahead_ref, behind_ref, grad_ref, loss_ref):
    side = side_ref[0].astype(F32)
    parcel = parcel_ref[...]
    grad, total = None, None
    for text_ref, place in ((own_ref, 0), (mate_ref, side), (ahead_ref, HALF), (behind_ref, -HALF)):
        text = text_ref[...]
        slope, loss = pair_terms(text, parcel, place)
        part = dot(slope, text, ((0,), (0,)))
        grad, total = (part, loss) if grad is None else (grad + part, total + loss)
    grad_ref[...] = grad
    loss_ref[...] = total


def image_end(
    side_ref, parcel_ref, far_ref, proj_ref, grad_ref, loss_ref, feats_ref, back_ref, terms_ref, out_loss_ref
):
    half = feats_ref.shape[1] // 2
    far = far_ref[...]
    slope, loss = pair_terms(far, parcel_ref[...], -side_ref[0].astype(F32))
    out_loss_ref[...] = loss_ref[...] + loss
    unit_grad = TEMP * (grad_ref[...] + dot(slope, far, ((0,), (0,))))
    proj = proj_ref[...]
    norm = jnp.sqrt(jnp.sum(proj * proj, axis=1, keepdims=True) + 1e-06)
    unit = proj / norm
    inner = jnp.sum(unit * unit_grad, axis=1, keepdims=True)
    back = ((unit_grad - unit * inner) / norm).astype(BF16)
    back_ref[...] = back
    terms_ref[:, :half] = dot(back, feats_ref[:, half:], ((0,), (0,))).astype(BF16)
    terms_ref[:, half:] = dot(back, feats_ref[:, :half], ((0,), (0,))).astype(BF16)


def text_side(side_ref, text_ref, mate_ref, own_ref, ahead_ref, behind_ref, grad_ref, mate_grad_ref):
    rows = text_ref.shape[0]
    side = side_ref[0].astype(F32)
    own, ahead, behind = own_ref[...], ahead_ref[...], behind_ref[...]
    near = jnp.where(side > 0, ahead, behind)

    def total(text, parcels):
        parts = [
            dot(pair_terms(text, parcel, place, with_loss=False), parcel[:rows], ((1,), (0,)))
            for parcel, place in parcels
        ]
        return sum(parts[1:], parts[0])

    mate_grad_ref[...] = total(mate_ref[...], [(own, side), (near, -side)]).astype(BF16)
    grad_ref[...] = total(text_ref[...], [(own, 0), (ahead, -HALF), (behind, HALF)])


def local(image_feats, text_emb, head_weight, partner):
    rows, width = image_feats.shape
    blocks = lax.axis_size(LOOP)
    core = lax.axis_index(CORE)
    here = lax.axis_index(LOOP).astype(jnp.int32).reshape(1)
    side = (1 - 2 * core).astype(jnp.int32).reshape(1)
    shape = jax.ShapeDtypeStruct
    product = 2 * rows * width * width
    pair = 2 * rows * rows * width

    ahead, behind = from_ahead(text_emb, HALF), from_ahead(text_emb, -HALF)
    mate = other_core(text_emb)

    proj, parcel = kernel_call(
        lambda *refs: prepare(blocks, *refs),
        [shape((rows, width), F32), shape((rows + TAIL, width), BF16)],
        [here, image_feats, head_weight, partner.reshape(1, rows)],
        product,
        1,
    )
    parcel_ahead, parcel_behind = from_ahead(parcel, HALF), from_ahead(parcel, -HALF)
    ahead, behind, parcel = lax.optimization_barrier((ahead, behind, parcel))
    far = other_core(jnp.where(core == 0, ahead, behind))
    grad, loss = kernel_call(
        image_start,
        [shape((rows, width), F32), shape((1, rows), F32)],
        [side, parcel, text_emb, mate, ahead, behind],
        0,
        1,
    )
    proj_grad, terms, row_loss = kernel_call(
        image_end,
        [shape((rows, width), BF16), shape((width, width), BF16), shape((1, rows), F32)],
        [side, parcel, far, proj, grad, loss, image_feats],
        0,
        1,
    )
    terms = after(terms, parcel_ahead, parcel_behind)

    n_col, n_row = lax.axis_size(COL), lax.axis_size(ROW)
    cols, tall = width // n_col, width // n_row
    mine = lax.all_to_all(terms.reshape(n_col, cols, width), COL, 0, 0, tiled=True)

    text_part, mate_part = kernel_call(
        text_side,
        [shape((rows, width), F32), shape((rows, width), BF16)],
        [side, after(text_emb, proj_grad), mate, parcel, parcel_ahead, parcel_behind],
        10 * pair,
        1,
    )
    text_grad = TEMP * (text_part + other_core(mate_part).astype(F32))
    feat_grad = dot(proj_grad, head_weight, ((1,), (1,))).astype(BF16)

    pick = jnp.tile(jnp.eye(cols, dtype=BF16), (n_col, 1))
    summed = dot(mine.reshape(width, width), pick, ((0,), (0,))).astype(BF16)
    order = [(i + n_row // 2) % n_row for i in range(n_row)]
    last = lax.all_to_all(
        summed.reshape(n_row, 2, tall * cols // 2), ROW, 0, 0, axis_index_groups=[order], tiled=True
    )
    head_grad = jnp.sum(last.astype(F32), axis=0).reshape(tall, cols)
    return row_loss.reshape(rows), feat_grad, text_grad, head_grad


def solution(mesh):
    n_row, n_col = mesh.devices.shape
    fine = Mesh(mesh.devices.reshape(n_row, n_col // CORES, CORES), LOOP)
    split = P(LOOP)
    return jax.shard_map(
        local,
        mesh=fine,
        in_specs=(P(LOOP, None), P(LOOP, None), P(), split),
        out_specs=(split, P(LOOP, None), P(LOOP, None), P(ROW, COL)),
        check_vma=False,
    )
```

```python
import jax
import jax.numpy as jnp
from jax import lax
from jax.experimental import pallas as pl
from jax.experimental.pallas import tpu as pltpu
from jax.sharding import Mesh, PartitionSpec as P

HALF = 2
TEMP = 10.0
BIAS = -4.0
CORES = 2
TAIL = 16
ROW, CHIP, CORE = "row", "chip", "core"
LOOP = (ROW, CHIP, CORE)
COL = (CHIP, CORE)
BF16 = jnp.bfloat16
F32 = jnp.float32
VMEM = pl.BlockSpec(memory_space=pltpu.VMEM)
SMEM = pl.BlockSpec(memory_space=pltpu.SMEM)


def from_ahead(block, distance):
    n = lax.axis_size(LOOP)
    return lax.ppermute(block, LOOP, [((i + distance) % n, i) for i in range(n)])


def other_core(block):
    return lax.ppermute(block, CORE, [(0, 1), (1, 0)])


def after(value, *earlier):
    return lax.optimization_barrier((value, *earlier))[0]


def dot(a, b, dims):
    return lax.dot_general(a, b, (dims, ((), ())), preferred_element_type=F32)


def kernel_call(body, outs, args, flops, scalars=0):
    moved = sum(a.size * a.dtype.itemsize for a in args)
    moved += sum(o.size * o.dtype.itemsize for o in outs)
    return pl.pallas_call(
        body,
        out_shape=outs,
        in_specs=[SMEM] * scalars + [VMEM] * (len(args) - scalars),
        out_specs=[VMEM] * len(outs),
        compiler_params=pltpu.CompilerParams(vmem_limit_bytes=16 * 2**20),
        cost_estimate=pl.CostEstimate(flops=flops, bytes_accessed=moved if flops else 0, transcendentals=0),
    )(*args)


def prepare(blocks, here_ref, feats_ref, weight_ref, partner_ref, proj_ref, parcel_ref):
    rows, width = feats_ref.shape
    proj = jnp.dot(feats_ref[...], weight_ref[...], preferred_element_type=F32)
    proj_ref[...] = proj
    norm = jnp.sqrt(jnp.sum(proj * proj, axis=1, keepdims=True) + 1e-06)
    parcel_ref[:rows, :] = (proj / norm).astype(BF16)
    partner = partner_ref[...]
    block = lax.div(partner, rows)
    place = block - here_ref[0] + HALF
    place = jnp.where(place < 0, place + blocks, place)
    place = jnp.where(place >= blocks, place - blocks, place)
    line = lax.broadcasted_iota(jnp.int32, (TAIL, rows), 0)
    codes = jnp.where(line == 0, place, jnp.where(line == 1, partner - block * rows, 0))
    parcel_ref[rows:, :] = jnp.zeros((TAIL, width), BF16)
    parcel_ref[rows:, :rows] = codes.astype(F32).astype(BF16)


def pair_terms(text, parcel, place, with_loss=True):
    rows = text.shape[0]
    codes = parcel[rows:, :rows].astype(F32)
    target = (codes[0:1] - (place + HALF)) * rows + codes[1:2]
    match = lax.broadcasted_iota(jnp.int32, (rows, rows), 0).astype(F32) == target
    logit = TEMP * dot(text, parcel[:rows], ((1,), (1,))) + BIAS
    z = jnp.where(match, -logit, logit)
    small = jnp.exp(-jnp.abs(z))
    share = 1.0 / (1.0 + small)
    sigmoid = jnp.where(z >= 0, share, small * share)
    slope = jnp.where(match, -sigmoid, sigmoid).astype(BF16)
    if not with_loss:
        return slope
    loss = jnp.sum(jnp.maximum(z, 0.0) + jnp.log1p(small), axis=0, keepdims=True)
    return slope, loss


def image_start(side_ref, parcel_ref, own_ref, mate_ref, ahead_ref, behind_ref, grad_ref, loss_ref):
    side = side_ref[0].astype(F32)
    parcel = parcel_ref[...]
    grad, total = None, None
    for text_ref, place in ((own_ref, 0), (mate_ref, side), (ahead_ref, HALF), (behind_ref, -HALF)):
        text = text_ref[...]
        slope, loss = pair_terms(text, parcel, place)
        part = dot(slope, text, ((0,), (0,)))
        grad, total = (part, loss) if grad is None else (grad + part, total + loss)
    grad_ref[...] = grad
    loss_ref[...] = total


def image_end(
    side_ref, parcel_ref, far_ref, proj_ref, grad_ref, loss_ref, feats_ref, back_ref, terms_ref, out_loss_ref
):
    half = feats_ref.shape[1] // 2
    far = far_ref[...]
    slope, loss = pair_terms(far, parcel_ref[...], -side_ref[0].astype(F32))
    out_loss_ref[...] = loss_ref[...] + loss
    unit_grad = TEMP * (grad_ref[...] + dot(slope, far, ((0,), (0,))))
    proj = proj_ref[...]
    norm = jnp.sqrt(jnp.sum(proj * proj, axis=1, keepdims=True) + 1e-06)
    unit = proj / norm
    inner = jnp.sum(unit * unit_grad, axis=1, keepdims=True)
    back = ((unit_grad - unit * inner) / norm).astype(BF16)
    back_ref[...] = back
    terms_ref[:, :half] = dot(back, feats_ref[:, half:], ((0,), (0,))).astype(BF16)
    terms_ref[:, half:] = dot(back, feats_ref[:, :half], ((0,), (0,))).astype(BF16)


def text_side(side_ref, text_ref, mate_ref, own_ref, ahead_ref, behind_ref, grad_ref, mate_grad_ref):
    rows = text_ref.shape[0]
    side = side_ref[0].astype(F32)
    own, ahead, behind = own_ref[...], ahead_ref[...], behind_ref[...]
    near = jnp.where(side > 0, ahead, behind)

    def total(text, parcels):
        parts = [
            dot(pair_terms(text, parcel, place, with_loss=False), parcel[:rows], ((1,), (0,)))
            for parcel, place in parcels
        ]
        return sum(parts[1:], parts[0])

    mate_grad_ref[...] = total(mate_ref[...], [(own, side), (near, -side)]).astype(BF16)
    grad_ref[...] = total(text_ref[...], [(own, 0), (ahead, -HALF), (behind, HALF)])


def local(image_feats, text_emb, head_weight, partner):
    rows, width = image_feats.shape
    blocks = lax.axis_size(LOOP)
    core = lax.axis_index(CORE)
    here = lax.axis_index(LOOP).astype(jnp.int32).reshape(1)
    side = (1 - 2 * core).astype(jnp.int32).reshape(1)
    shape = jax.ShapeDtypeStruct
    product = 2 * rows * width * width
    pair = 2 * rows * rows * width

    ahead, behind = from_ahead(text_emb, HALF), from_ahead(text_emb, -HALF)
    mate = other_core(text_emb)

    proj, parcel = kernel_call(
        lambda *refs: prepare(blocks, *refs),
        [shape((rows, width), F32), shape((rows + TAIL, width), BF16)],
        [here, image_feats, head_weight, partner.reshape(1, rows)],
        product,
        1,
    )
    ahead, behind, parcel = lax.optimization_barrier((ahead, behind, parcel))
    near = jnp.where(core == 0, ahead, behind)
    far = other_core(near)
    sent = after(parcel, near)
    parcel_ahead, parcel_behind = from_ahead(sent, HALF), from_ahead(sent, -HALF)
    grad, loss = kernel_call(
        image_start,
        [shape((rows, width), F32), shape((1, rows), F32)],
        [side, parcel, text_emb, mate, ahead, behind],
        8 * pair,
        1,
    )
    proj_grad, terms, row_loss = kernel_call(
        image_end,
        [shape((rows, width), BF16), shape((width, width), BF16), shape((1, rows), F32)],
        [side, parcel, far, proj, grad, loss, image_feats],
        2 * pair + product,
        1,
    )
    terms = after(terms, parcel_ahead, parcel_behind)

    n_col, n_row = lax.axis_size(COL), lax.axis_size(ROW)
    cols, tall = width // n_col, width // n_row
    mine = lax.all_to_all(terms.reshape(n_col, cols, width), COL, 0, 0, tiled=True)

    text_part, mate_part = kernel_call(
        text_side,
        [shape((rows, width), F32), shape((rows, width), BF16)],
        [side, after(text_emb, proj_grad), mate, parcel, parcel_ahead, parcel_behind],
        10 * pair,
        1,
    )
    text_grad = TEMP * (text_part + other_core(mate_part).astype(F32))
    feat_grad = dot(proj_grad, head_weight, ((1,), (1,))).astype(BF16)

    pick = jnp.tile(jnp.eye(cols, dtype=BF16), (n_col, 1))
    summed = dot(mine.reshape(width, width), pick, ((0,), (0,))).astype(BF16)
    order = [(i + n_row // 2) % n_row for i in range(n_row)]
    last = lax.all_to_all(
        summed.reshape(n_row, 2, tall * cols // 2), ROW, 0, 0, axis_index_groups=[order], tiled=True
    )
    head_grad = jnp.sum(last.astype(F32), axis=0).reshape(tall, cols)
    return row_loss.reshape(rows), feat_grad, text_grad, head_grad


def solution(mesh):
    n_row, n_col = mesh.devices.shape
    fine = Mesh(mesh.devices.reshape(n_row, n_col // CORES, CORES), LOOP)
    split = P(LOOP)
    return jax.shard_map(
        local,
        mesh=fine,
        in_specs=(P(LOOP, None), P(LOOP, None), P(), split),
        out_specs=(split, P(LOOP, None), P(LOOP, None), P(ROW, COL)),
        check_vma=False,
    )
```

```python
import jax
import jax.numpy as jnp
from jax import lax
from jax.experimental import pallas as pl
from jax.experimental.pallas import tpu as pltpu
from jax.sharding import Mesh, PartitionSpec as P

HALF = 2
TEMP = 10.0
BIAS = -4.0
CORES = 2
TAIL = 16
ROW, CHIP, CORE = "row", "chip", "core"
LOOP = (ROW, CHIP, CORE)
COL = (CHIP, CORE)
BF16 = jnp.bfloat16
F32 = jnp.float32
VMEM = pl.BlockSpec(memory_space=pltpu.VMEM)
SMEM = pl.BlockSpec(memory_space=pltpu.SMEM)


def from_ahead(block, distance):
    n = lax.axis_size(LOOP)
    return lax.ppermute(block, LOOP, [((i + distance) % n, i) for i in range(n)])


def other_core(block):
    return lax.ppermute(block, CORE, [(0, 1), (1, 0)])


def after(value, *earlier):
    return lax.optimization_barrier((value, *earlier))[0]


def dot(a, b, dims):
    return lax.dot_general(a, b, (dims, ((), ())), preferred_element_type=F32)


def kernel_call(body, outs, args, flops, scalars=0):
    moved = sum(a.size * a.dtype.itemsize for a in args)
    moved += sum(o.size * o.dtype.itemsize for o in outs)
    return pl.pallas_call(
        body,
        out_shape=outs,
        in_specs=[SMEM] * scalars + [VMEM] * (len(args) - scalars),
        out_specs=[VMEM] * len(outs),
        compiler_params=pltpu.CompilerParams(vmem_limit_bytes=16 * 2**20),
        cost_estimate=pl.CostEstimate(flops=flops, bytes_accessed=moved if flops else 0, transcendentals=0),
    )(*args)


def prepare(blocks, here_ref, feats_ref, weight_ref, partner_ref, proj_ref, parcel_ref):
    rows, width = feats_ref.shape
    proj = jnp.dot(feats_ref[...], weight_ref[...], preferred_element_type=F32)
    proj_ref[...] = proj
    norm = jnp.sqrt(jnp.sum(proj * proj, axis=1, keepdims=True) + 1e-06)
    parcel_ref[:rows, :] = (proj / norm).astype(BF16)
    partner = partner_ref[...]
    block = lax.div(partner, rows)
    place = block - here_ref[0] + HALF
    place = jnp.where(place < 0, place + blocks, place)
    place = jnp.where(place >= blocks, place - blocks, place)
    line = lax.broadcasted_iota(jnp.int32, (TAIL, rows), 0)
    codes = jnp.where(line == 0, place, jnp.where(line == 1, partner - block * rows, 0))
    parcel_ref[rows:, :] = jnp.zeros((TAIL, width), BF16)
    parcel_ref[rows:, :rows] = codes.astype(F32).astype(BF16)


def pair_terms(text, parcel, place, with_loss=True):
    rows = text.shape[0]
    codes = parcel[rows:, :rows].astype(F32)
    target = (codes[0:1] - (place + HALF)) * rows + codes[1:2]
    match = lax.broadcasted_iota(jnp.int32, (rows, rows), 0).astype(F32) == target
    logit = TEMP * dot(text, parcel[:rows], ((1,), (1,))) + BIAS
    z = jnp.where(match, -logit, logit)
    small = jnp.exp(-jnp.abs(z))
    share = 1.0 / (1.0 + small)
    sigmoid = jnp.where(z >= 0, share, small * share)
    slope = jnp.where(match, -sigmoid, sigmoid).astype(BF16)
    if not with_loss:
        return slope
    loss = jnp.sum(jnp.maximum(z, 0.0) + jnp.log1p(small), axis=0, keepdims=True)
    return slope, loss


def image_start(side_ref, parcel_ref, own_ref, mate_ref, ahead_ref, behind_ref, grad_ref, loss_ref):
    side = side_ref[0].astype(F32)
    parcel = parcel_ref[...]
    grad, total = None, None
    for text_ref, place in ((own_ref, 0), (mate_ref, side), (ahead_ref, HALF), (behind_ref, -HALF)):
        text = text_ref[...]
        slope, loss = pair_terms(text, parcel, place)
        part = dot(slope, text, ((0,), (0,)))
        grad, total = (part, loss) if grad is None else (grad + part, total + loss)
    grad_ref[...] = grad
    loss_ref[...] = total


def image_end(
    side_ref, parcel_ref, far_ref, proj_ref, grad_ref, loss_ref, feats_ref, back_ref, terms_ref, out_loss_ref
):
    half = feats_ref.shape[1] // 2
    far = far_ref[...]
    slope, loss = pair_terms(far, parcel_ref[...], -side_ref[0].astype(F32))
    out_loss_ref[...] = loss_ref[...] + loss
    unit_grad = TEMP * (grad_ref[...] + dot(slope, far, ((0,), (0,))))
    proj = proj_ref[...]
    norm = jnp.sqrt(jnp.sum(proj * proj, axis=1, keepdims=True) + 1e-06)
    unit = proj / norm
    inner = jnp.sum(unit * unit_grad, axis=1, keepdims=True)
    back = ((unit_grad - unit * inner) / norm).astype(BF16)
    back_ref[...] = back
    terms_ref[:, :half] = dot(back, feats_ref[:, half:], ((0,), (0,))).astype(BF16)
    terms_ref[:, half:] = dot(back, feats_ref[:, :half], ((0,), (0,))).astype(BF16)


def text_side(side_ref, text_ref, mate_ref, own_ref, ahead_ref, behind_ref, grad_ref, mate_grad_ref):
    rows = text_ref.shape[0]
    side = side_ref[0].astype(F32)
    own, ahead, behind = own_ref[...], ahead_ref[...], behind_ref[...]
    near = jnp.where(side > 0, ahead, behind)

    def total(text, parcels):
        parts = [
            dot(pair_terms(text, parcel, place, with_loss=False), parcel[:rows], ((1,), (0,)))
            for parcel, place in parcels
        ]
        return sum(parts[1:], parts[0])

    mate_grad_ref[...] = total(mate_ref[...], [(own, side), (near, -side)]).astype(BF16)
    grad_ref[...] = total(text_ref[...], [(own, 0), (ahead, -HALF), (behind, HALF)])


def local(image_feats, text_emb, head_weight, partner):
    rows, width = image_feats.shape
    blocks = lax.axis_size(LOOP)
    core = lax.axis_index(CORE)
    here = lax.axis_index(LOOP).astype(jnp.int32).reshape(1)
    side = (1 - 2 * core).astype(jnp.int32).reshape(1)
    shape = jax.ShapeDtypeStruct
    product = 2 * rows * width * width
    pair = 2 * rows * rows * width

    ahead, behind = from_ahead(text_emb, HALF), from_ahead(text_emb, -HALF)
    mate = other_core(text_emb)

    proj, parcel = kernel_call(
        lambda *refs: prepare(blocks, *refs),
        [shape((rows, width), F32), shape((rows + TAIL, width), BF16)],
        [here, image_feats, head_weight, partner.reshape(1, rows)],
        product,
        1,
    )
    ahead, behind, parcel = lax.optimization_barrier((ahead, behind, parcel))
    near = jnp.where(core == 0, ahead, behind)
    far = other_core(near)
    grad, loss = kernel_call(
        image_start,
        [shape((rows, width), F32), shape((1, rows), F32)],
        [side, parcel, text_emb, mate, ahead, behind],
        8 * pair,
        1,
    )
    proj_grad, terms, row_loss = kernel_call(
        image_end,
        [shape((rows, width), BF16), shape((width, width), BF16), shape((1, rows), F32)],
        [side, parcel, far, proj, grad, loss, image_feats],
        2 * pair + product,
        1,
    )
    n_col, n_row = lax.axis_size(COL), lax.axis_size(ROW)
    cols, tall = width // n_col, width // n_row
    mine = lax.all_to_all(terms.reshape(n_col, cols, width), COL, 0, 0, tiled=True)

    feat_grad = dot(proj_grad, head_weight, ((1,), (1,))).astype(BF16)

    pick = jnp.tile(jnp.eye(cols, dtype=BF16), (n_col, 1))
    pick = after(pick, feat_grad)
    summed = dot(mine.reshape(width, width), pick, ((0,), (0,))).astype(BF16)
    order = [(i + n_row // 2) % n_row for i in range(n_row)]
    last = lax.all_to_all(
        summed.reshape(n_row, 2, tall * cols // 2), ROW, 0, 0, axis_index_groups=[order], tiled=True
    )
    sent = after(parcel, summed)
    parcel_ahead, parcel_behind = from_ahead(sent, HALF), from_ahead(sent, -HALF)
    text_part, mate_part = kernel_call(
        text_side,
        [shape((rows, width), F32), shape((rows, width), BF16)],
        [side, text_emb, mate, parcel, parcel_ahead, parcel_behind],
        10 * pair,
        1,
    )
    text_grad = TEMP * (text_part + other_core(mate_part).astype(F32))

    head_grad = jnp.sum(last.astype(F32), axis=0).reshape(tall, cols)
    return row_loss.reshape(rows), feat_grad, text_grad, head_grad


def solution(mesh):
    n_row, n_col = mesh.devices.shape
    fine = Mesh(mesh.devices.reshape(n_row, n_col // CORES, CORES), LOOP)
    split = P(LOOP)
    return jax.shard_map(
        local,
        mesh=fine,
        in_specs=(P(LOOP, None), P(LOOP, None), P(), split),
        out_specs=(split, P(LOOP, None), P(LOOP, None), P(ROW, COL)),
        check_vma=False,
    )
```

```python
import jax
import jax.numpy as jnp
from jax import lax
from jax.experimental import pallas as pl
from jax.experimental.pallas import tpu as pltpu
from jax.sharding import Mesh, PartitionSpec as P

HALF = 2
TEMP = 10.0
BIAS = -4.0
CORES = 2
TAIL = 16
ROW, CHIP, CORE = "row", "chip", "core"
LOOP = (ROW, CHIP, CORE)
COL = (CHIP, CORE)
BF16 = jnp.bfloat16
F32 = jnp.float32
VMEM = pl.BlockSpec(memory_space=pltpu.VMEM)
SMEM = pl.BlockSpec(memory_space=pltpu.SMEM)


def from_ahead(block, distance):
    n = lax.axis_size(LOOP)
    return lax.ppermute(block, LOOP, [((i + distance) % n, i) for i in range(n)])


def other_core(block):
    return lax.ppermute(block, CORE, [(0, 1), (1, 0)])


def after(value, *earlier):
    return lax.optimization_barrier((value, *earlier))[0]


def dot(a, b, dims):
    return lax.dot_general(a, b, (dims, ((), ())), preferred_element_type=F32)


def kernel_call(body, outs, args, flops, scalars=0):
    moved = sum(a.size * a.dtype.itemsize for a in args)
    moved += sum(o.size * o.dtype.itemsize for o in outs)
    return pl.pallas_call(
        body,
        out_shape=outs,
        in_specs=[SMEM] * scalars + [VMEM] * (len(args) - scalars),
        out_specs=[VMEM] * len(outs),
        compiler_params=pltpu.CompilerParams(vmem_limit_bytes=32 * 2**20),
        cost_estimate=pl.CostEstimate(flops=flops, bytes_accessed=moved, transcendentals=0),
    )(*args)


def prepare(blocks, here_ref, feats_ref, weight_ref, partner_ref, proj_ref, parcel_ref):
    rows, width = feats_ref.shape
    proj = jnp.dot(feats_ref[...], weight_ref[...], preferred_element_type=F32)
    proj_ref[...] = proj
    norm = jnp.sqrt(jnp.sum(proj * proj, axis=1, keepdims=True) + 1e-06)
    parcel_ref[:rows, :] = (proj / norm).astype(BF16)
    partner = partner_ref[...]
    block = lax.div(partner, rows)
    place = block - here_ref[0] + HALF
    place = jnp.where(place < 0, place + blocks, place)
    place = jnp.where(place >= blocks, place - blocks, place)
    line = lax.broadcasted_iota(jnp.int32, (TAIL, rows), 0)
    codes = jnp.where(line == 0, place, jnp.where(line == 1, partner - block * rows, 0))
    parcel_ref[rows:, :] = jnp.zeros((TAIL, width), BF16)
    parcel_ref[rows:, :rows] = codes.astype(F32).astype(BF16)


def pair_terms(text, parcel_ref, place, with_loss=True):
    rows = text.shape[0]
    codes = parcel_ref[rows:, :rows].astype(F32)
    target = (codes[0:1] - (place + HALF)) * rows + codes[1:2]
    match = lax.broadcasted_iota(jnp.int32, (rows, rows), 0).astype(F32) == target
    logit = TEMP * dot(text, parcel_ref[:rows, :], ((1,), (1,))) + BIAS
    z = jnp.where(match, -logit, logit)
    small = jnp.exp(-jnp.abs(z))
    share = 1.0 / (1.0 + small)
    sigmoid = jnp.where(z >= 0, share, small * share)
    slope = jnp.where(match, -sigmoid, sigmoid).astype(BF16)
    if not with_loss:
        return slope
    loss = jnp.sum(jnp.maximum(z, 0.0) + jnp.log1p(small), axis=0, keepdims=True)
    return slope, loss


def image_start(side_ref, parcel_ref, own_ref, mate_ref, ahead_ref, behind_ref, grad_ref, loss_ref):
    side = side_ref[0].astype(F32)
    grad, total = None, None
    for text_ref, place in ((own_ref, 0), (mate_ref, side), (ahead_ref, HALF), (behind_ref, -HALF)):
        text = text_ref[...]
        slope, loss = pair_terms(text, parcel_ref, place)
        part = dot(slope, text, ((0,), (0,)))
        grad, total = (part, loss) if grad is None else (grad + part, total + loss)
    grad_ref[...] = grad
    loss_ref[...] = total


def image_end(
    side_ref, parcel_ref, far_ref, proj_ref, grad_ref, loss_ref, feats_ref, back_ref, terms_ref, out_loss_ref
):
    half = feats_ref.shape[1] // 2
    far = far_ref[...]
    slope, loss = pair_terms(far, parcel_ref, -side_ref[0].astype(F32))
    out_loss_ref[...] = loss_ref[...] + loss
    unit_grad = TEMP * (grad_ref[...] + dot(slope, far, ((0,), (0,))))
    proj = proj_ref[...]
    norm = jnp.sqrt(jnp.sum(proj * proj, axis=1, keepdims=True) + 1e-06)
    unit = proj / norm
    inner = jnp.sum(unit * unit_grad, axis=1, keepdims=True)
    back = ((unit_grad - unit * inner) / norm).astype(BF16)
    back_ref[...] = back
    terms_ref[:, :half] = dot(back, feats_ref[:, half:], ((0,), (0,))).astype(BF16)
    terms_ref[:, half:] = dot(back, feats_ref[:, :half], ((0,), (0,))).astype(BF16)


def text_side(side_ref, text_ref, own_ref, mate_ref, ahead_ref, behind_ref, far_ref, grad_ref):
    rows = text_ref.shape[0]
    side = side_ref[0].astype(F32)
    text = text_ref[...]
    grad = None
    for parcel_ref, place in ((own_ref, 0), (mate_ref, -side), (ahead_ref, -HALF), (behind_ref, HALF), (far_ref, side)):
        slope = pair_terms(text, parcel_ref, place, with_loss=False)
        part = dot(slope, parcel_ref[:rows, :], ((1,), (0,)))
        grad = part if grad is None else grad + part
    grad_ref[...] = TEMP * grad


def local(image_feats, text_emb, head_weight, partner):
    rows, width = image_feats.shape
    blocks = lax.axis_size(LOOP)
    core = lax.axis_index(CORE)
    here = lax.axis_index(LOOP).astype(jnp.int32).reshape(1)
    side = (1 - 2 * core).astype(jnp.int32).reshape(1)
    shape = jax.ShapeDtypeStruct
    product = 2 * rows * width * width
    pair = 2 * rows * rows * width

    ahead, behind = from_ahead(text_emb, HALF), from_ahead(text_emb, -HALF)
    mate = other_core(text_emb)

    proj, parcel = kernel_call(
        lambda *refs: prepare(blocks, *refs),
        [shape((rows, width), F32), shape((rows + TAIL, width), BF16)],
        [here, image_feats, head_weight, partner.reshape(1, rows)],
        product,
        1,
    )
    ahead, behind, parcel = lax.optimization_barrier((ahead, behind, parcel))
    far = other_core(jnp.where(core == 0, ahead, behind))
    grad, loss = kernel_call(
        image_start,
        [shape((rows, width), F32), shape((1, rows), F32)],
        [side, parcel, text_emb, mate, ahead, behind],
        8 * pair,
        1,
    )
    proj_grad, terms, row_loss = kernel_call(
        image_end,
        [shape((rows, width), BF16), shape((width, width), BF16), shape((1, rows), F32)],
        [side, parcel, far, proj, grad, loss, image_feats],
        2 * pair + product,
        1,
    )
    sent = after(parcel, terms)
    parcel_ahead, parcel_behind = from_ahead(sent, HALF), from_ahead(sent, -HALF)
    parcel_mate = other_core(sent)
    parcel_far = other_core(jnp.where(core == 0, parcel_ahead, parcel_behind))

    n_col, n_row = lax.axis_size(COL), lax.axis_size(ROW)
    cols, tall = width // n_col, width // n_row
    mine = lax.all_to_all(terms.reshape(n_col, cols, width), COL, 0, 0, tiled=True)

    (text_grad,) = kernel_call(
        text_side,
        [shape((rows, width), F32)],
        [side, text_emb, parcel, parcel_mate, parcel_ahead, parcel_behind, parcel_far],
        10 * pair,
        1,
    )
    feat_grad = dot(proj_grad, head_weight, ((1,), (1,))).astype(BF16)

    pick = jnp.tile(jnp.eye(cols, dtype=BF16), (n_col, 1))
    summed = dot(mine.reshape(width, width), pick, ((0,), (0,))).astype(BF16)
    order = [(i + n_row // 2) % n_row for i in range(n_row)]
    last = lax.all_to_all(
        summed.reshape(n_row, 2, tall * cols // 2), ROW, 0, 0, axis_index_groups=[order], tiled=True
    )
    head_grad = jnp.sum(last.astype(F32), axis=0).reshape(tall, cols)
    return row_loss.reshape(rows), feat_grad, text_grad, head_grad


def solution(mesh):
    n_row, n_col = mesh.devices.shape
    fine = Mesh(mesh.devices.reshape(n_row, n_col // CORES, CORES), LOOP)
    split = P(LOOP)
    return jax.shard_map(
        local,
        mesh=fine,
        in_specs=(P(LOOP, None), P(LOOP, None), P(), split),
        out_specs=(split, P(LOOP, None), P(LOOP, None), P(ROW, COL)),
        check_vma=False,
    )
```

```python
import jax
import jax.numpy as jnp
from jax import lax
from jax.experimental import pallas as pl
from jax.experimental.pallas import tpu as pltpu
from jax.sharding import Mesh, PartitionSpec as P

HALF = 2
TEMP = 10.0
BIAS = -4.0
CORES = 2
TAIL = 16
ROW, CHIP, CORE = "row", "chip", "core"
LOOP = (ROW, CHIP, CORE)
COL = (CHIP, CORE)
BF16 = jnp.bfloat16
F32 = jnp.float32
VMEM = pl.BlockSpec(memory_space=pltpu.VMEM)
SMEM = pl.BlockSpec(memory_space=pltpu.SMEM)


def from_ahead(block, distance):
    n = lax.axis_size(LOOP)
    return lax.ppermute(block, LOOP, [((i + distance) % n, i) for i in range(n)])


def other_core(block):
    return lax.ppermute(block, CORE, [(0, 1), (1, 0)])


def after(value, *earlier):
    return lax.optimization_barrier((value, *earlier))[0]


def dot(a, b, dims):
    return lax.dot_general(a, b, (dims, ((), ())), preferred_element_type=F32)


def kernel_call(body, outs, args, flops, scalars=0):
    moved = sum(a.size * a.dtype.itemsize for a in args)
    moved += sum(o.size * o.dtype.itemsize for o in outs)
    return pl.pallas_call(
        body,
        out_shape=outs,
        in_specs=[SMEM] * scalars + [VMEM] * (len(args) - scalars),
        out_specs=[VMEM] * len(outs),
        compiler_params=pltpu.CompilerParams(vmem_limit_bytes=32 * 2**20),
        cost_estimate=pl.CostEstimate(flops=flops, bytes_accessed=moved, transcendentals=0),
    )(*args)


def prepare(blocks, here_ref, feats_ref, weight_ref, partner_ref, proj_ref, parcel_ref):
    rows, width = feats_ref.shape
    proj = jnp.dot(feats_ref[...], weight_ref[...], preferred_element_type=F32)
    proj_ref[...] = proj
    norm = jnp.sqrt(jnp.sum(proj * proj, axis=1, keepdims=True) + 1e-06)
    parcel_ref[:rows, :] = (proj / norm).astype(BF16)
    partner = partner_ref[...]
    block = lax.div(partner, rows)
    place = block - here_ref[0] + HALF
    place = jnp.where(place < 0, place + blocks, place)
    place = jnp.where(place >= blocks, place - blocks, place)
    line = lax.broadcasted_iota(jnp.int32, (TAIL, rows), 0)
    codes = jnp.where(line == 0, place, jnp.where(line == 1, partner - block * rows, 0))
    parcel_ref[rows:, :] = jnp.zeros((TAIL, width), BF16)
    parcel_ref[rows:, :rows] = codes.astype(F32).astype(BF16)


def pair_terms(text, parcel_ref, place, with_loss=True):
    rows = text.shape[0]
    codes = parcel_ref[rows:, :rows].astype(F32)
    target = (codes[0:1] - (place + HALF)) * rows + codes[1:2]
    match = lax.broadcasted_iota(jnp.int32, (rows, rows), 0).astype(F32) == target
    logit = TEMP * dot(text, parcel_ref[:rows, :], ((1,), (1,))) + BIAS
    z = jnp.where(match, -logit, logit)
    small = jnp.exp(-jnp.abs(z))
    share = 1.0 / (1.0 + small)
    sigmoid = jnp.where(z >= 0, share, small * share)
    slope = jnp.where(match, -sigmoid, sigmoid).astype(BF16)
    if not with_loss:
        return slope
    loss = jnp.sum(jnp.maximum(z, 0.0) + jnp.log1p(small), axis=0, keepdims=True)
    return slope, loss


def image_start(side_ref, parcel_ref, own_ref, mate_ref, ahead_ref, behind_ref, grad_ref, loss_ref):
    side = side_ref[0].astype(F32)
    grad, total = None, None
    for text_ref, place in ((own_ref, 0), (mate_ref, side), (ahead_ref, HALF), (behind_ref, -HALF)):
        text = text_ref[...]
        slope, loss = pair_terms(text, parcel_ref, place)
        part = dot(slope, text, ((0,), (0,)))
        grad, total = (part, loss) if grad is None else (grad + part, total + loss)
    grad_ref[...] = grad
    loss_ref[...] = total


def image_end(
    side_ref, parcel_ref, far_ref, proj_ref, grad_ref, loss_ref, feats_ref, back_ref, terms_ref, out_loss_ref
):
    half = feats_ref.shape[1] // 2
    far = far_ref[...]
    slope, loss = pair_terms(far, parcel_ref, -side_ref[0].astype(F32))
    out_loss_ref[...] = loss_ref[...] + loss
    unit_grad = TEMP * (grad_ref[...] + dot(slope, far, ((0,), (0,))))
    proj = proj_ref[...]
    norm = jnp.sqrt(jnp.sum(proj * proj, axis=1, keepdims=True) + 1e-06)
    unit = proj / norm
    inner = jnp.sum(unit * unit_grad, axis=1, keepdims=True)
    back = ((unit_grad - unit * inner) / norm).astype(BF16)
    back_ref[...] = back
    terms_ref[:, :half] = dot(back, feats_ref[:, half:], ((0,), (0,))).astype(BF16)
    terms_ref[:, half:] = dot(back, feats_ref[:, :half], ((0,), (0,))).astype(BF16)


def text_side(side_ref, text_ref, own_ref, mate_ref, ahead_ref, behind_ref, far_ref, grad_ref):
    rows = text_ref.shape[0]
    side = side_ref[0].astype(F32)
    text = text_ref[...]
    grad = None
    for parcel_ref, place in ((own_ref, 0), (mate_ref, -side), (ahead_ref, -HALF), (behind_ref, HALF), (far_ref, side)):
        slope = pair_terms(text, parcel_ref, place, with_loss=False)
        part = dot(slope, parcel_ref[:rows, :], ((1,), (0,)))
        grad = part if grad is None else grad + part
    grad_ref[...] = TEMP * grad


def local(image_feats, text_emb, head_weight, partner):
    rows, width = image_feats.shape
    blocks = lax.axis_size(LOOP)
    core = lax.axis_index(CORE)
    here = lax.axis_index(LOOP).astype(jnp.int32).reshape(1)
    side = (1 - 2 * core).astype(jnp.int32).reshape(1)
    shape = jax.ShapeDtypeStruct
    product = 2 * rows * width * width
    pair = 2 * rows * rows * width

    ahead, behind = from_ahead(text_emb, HALF), from_ahead(text_emb, -HALF)
    mate = other_core(text_emb)

    proj, parcel = kernel_call(
        lambda *refs: prepare(blocks, *refs),
        [shape((rows, width), F32), shape((rows + TAIL, width), BF16)],
        [here, image_feats, head_weight, partner.reshape(1, rows)],
        product,
        1,
    )
    ahead, behind, parcel = lax.optimization_barrier((ahead, behind, parcel))
    far = other_core(jnp.where(core == 0, ahead, behind))
    grad, loss = kernel_call(
        image_start,
        [shape((rows, width), F32), shape((1, rows), F32)],
        [side, parcel, text_emb, mate, ahead, behind],
        8 * pair,
        1,
    )
    proj_grad, terms, row_loss = kernel_call(
        image_end,
        [shape((rows, width), BF16), shape((width, width), BF16), shape((1, rows), F32)],
        [side, parcel, far, proj, grad, loss, image_feats],
        2 * pair + product,
        1,
    )
    sent = after(parcel, terms)
    parcel_ahead, parcel_behind = from_ahead(sent, HALF), from_ahead(sent, -HALF)
    parcel_mate = other_core(sent)
    parcel_far = other_core(jnp.where(core == 0, parcel_ahead, parcel_behind))

    n_col, n_row = lax.axis_size(COL), lax.axis_size(ROW)
    cols, tall = width // n_col, width // n_row
    mine = lax.all_to_all(terms.reshape(n_col, cols, width), COL, 0, 0, tiled=True)

    (text_grad,) = kernel_call(
        text_side,
        [shape((rows, width), F32)],
        [side, text_emb, parcel, parcel_mate, parcel_ahead, parcel_behind, parcel_far],
        10 * pair,
        1,
    )
    feat_grad = dot(proj_grad, head_weight, ((1,), (1,))).astype(BF16)

    pick = jnp.tile(jnp.eye(cols, dtype=BF16), (n_col, 1))
    pick = after(pick, feat_grad)
    summed = dot(mine.reshape(width, width), pick, ((0,), (0,))).astype(BF16)
    order = [(i + n_row // 2) % n_row for i in range(n_row)]
    last = lax.all_to_all(
        summed.reshape(n_row, 2, tall * cols // 2), ROW, 0, 0, axis_index_groups=[order], tiled=True
    )
    head_grad = jnp.sum(last.astype(F32), axis=0).reshape(tall, cols)
    return row_loss.reshape(rows), feat_grad, text_grad, head_grad


def solution(mesh):
    n_row, n_col = mesh.devices.shape
    fine = Mesh(mesh.devices.reshape(n_row, n_col // CORES, CORES), LOOP)
    split = P(LOOP)
    return jax.shard_map(
        local,
        mesh=fine,
        in_specs=(P(LOOP, None), P(LOOP, None), P(), split),
        out_specs=(split, P(LOOP, None), P(LOOP, None), P(ROW, COL)),
        check_vma=False,
    )
```
